32 devices in a mesh: groups: 2 (over y), dp: 4 (over z), mp: 2 (over x), sub: 2 (over core).
Axes of the slice: x: 2, y: 2, z: 4, core: 2. Of those that a mesh axis runs over, the one named last changes fastest.
Arguments:
- example_blocks: int32 [32], P(('groups', 'dp')), parts along dimension 0, may hold values from 1 to 19, as said below
- layer_input: bfloat16 [4224, 4096], P(('groups', 'dp'), ('mp', 'sub')), parts along dimension 0, may hold values from -6 to 6
- out_grad: bfloat16 [4224, 4096], P(('groups', 'dp'), ('mp', 'sub')), parts along dimension 0, may hold values from -6 to 6
- gate_pre: bfloat16 [4224, 14336], P(('groups', 'dp'), ('mp', 'sub')), parts along dimension 0, may hold values from -6 to 6
- up_pre: bfloat16 [4224, 14336], P(('groups', 'dp'), ('mp', 'sub')), parts along dimension 0, may hold values from -6 to 6
- down_weight: bfloat16 [14336, 4096], P(('mp', 'sub'), 'dp'), may hold values from -0.046875 to 0.046875
- proj_input: bfloat16 [4096, 64], P(('mp', 'sub')), may hold values from -0.09375 to 0.09375
- proj_output: bfloat16 [4096, 64], P(('mp', 'sub')), may hold values from -0.09375 to 0.09375
- proj_hidden: bfloat16 [14336, 64], P(('mp', 'sub')), may hold values from -0.046875 to 0.046875
- proj_gate: bfloat16 [14336, 64], P(('mp', 'sub')), may hold values from -0.046875 to 0.046875
- proj_up: bfloat16 [14336, 64], P(('mp', 'sub')), may hold values from -0.046875 to 0.046875
Outputs:
- proj_grads: float32 [32, 12288], P(('groups', 'dp'), ('mp', 'sub')), parts along dimension 0
The draws below stay inside these ranges and needn't reach their ends.
There are 2 independent parts, one for each index of `groups`. The reference program is written for one: setup_inputs(seed, part) draws one part's arguments, and reference() takes and returns one part's arrays. A program takes and returns all parts, laid end to end along the dimension named above; an argument that names none is the same for every part. Nothing has to cross between parts.
Inputs may be any that keep to these rules, and one draw needn't show every extreme that they name: `example_blocks`: the entries of one data shard's 4 examples sum to at most 22, exactly 22 on some shard, and all entries together sum to exactly 13 times the number of data shards.
All inputs are finite; a program needn't handle non-finite values.
Results may differ from the reference program's by a relative error of at most 0.0041.
Values may be sent and summed in bfloat16 or wider, within the bound.
A program may use at most 128 MiB of HBM per device.

```python
import jax
import jax.numpy as jnp
from jax import lax

D = 4096
FF = 14336
K = 64
BLK = 24
EX_DEV = 4
RECV = 13
SLOTS = 22
EXAMPLES = 16
HOME_ROWS = 2112


def draw_example_blocks(key, part):
    key = jax.random.fold_in(key, 7)
    key_spread, key_order, key_weight = jax.random.split(key, 3)
    shards = EXAMPLES // EX_DEV
    halves = shards // 2
    spread = jax.random.randint(key_spread, (halves,), 0, RECV - EX_DEV + 1)
    spread = spread.at[0].set(RECV - EX_DEV)
    signed = jnp.concatenate([spread, -spread])
    order = jax.random.permutation(key_order, shards)
    shard_loads = RECV + signed[order]
    weights = jax.random.randint(key_weight, (shards, EX_DEV), 1, 5)
    extra = shard_loads - EX_DEV
    shares = extra[:, None] * weights // jnp.sum(weights, axis=1, keepdims=True)
    busiest = shard_loads == SLOTS
    shares = jnp.where(busiest[:, None], 0, shares)
    shares = shares.at[:, -1].add(extra - jnp.sum(shares, axis=1))
    return (1 + shares).reshape(EXAMPLES).astype(jnp.int32)


def steps_of(key, shape, pieces, smallest, high):
    level, own = 1.0, jax.random.fold_in(key, 6)
    for axis_at, blocks in pieces:
        draws = jnp.exp(jax.random.uniform(jax.random.fold_in(own, axis_at), (blocks,), jnp.float32, smallest / len(pieces), high / len(pieces)))
        level = level * jnp.repeat(draws, shape[axis_at] // blocks).reshape([-1 if axis == axis_at else 1 for axis in range(len(shape))])
    return level


def noise(own_key, dims, scale, limit, cuts=(), kind=jnp.bfloat16):
    loudness = steps_of(own_key, dims, cuts, -0.22, 0.18) if cuts else 1.0
    array = jax.random.normal(own_key, dims, jnp.float32) * scale * loudness
    return jnp.minimum(jnp.maximum(array, -limit), limit).astype(kind)


def setup_inputs(seed: int = 0, part: int = 0) -> dict:
    arg_keys = jax.random.split(jax.random.key(seed), 12)
    part_keys = jax.random.split(jax.random.fold_in(arg_keys[11], part), 12)
    return {
        "example_blocks": draw_example_blocks(jax.random.fold_in(jax.random.fold_in(arg_keys[11], part), 71), part),
        "layer_input": noise(part_keys[1], (HOME_ROWS, D), 1.0, 6.0, ((0, 4), (1, 4))),
        "out_grad": noise(part_keys[2], (HOME_ROWS, D), 1.0, 6.0, ((0, 4), (1, 4))),
        "gate_pre": noise(part_keys[3], (HOME_ROWS, FF), 1.0, 6.0, ((0, 4), (1, 4))),
        "up_pre": noise(part_keys[4], (HOME_ROWS, FF), 1.0, 6.0, ((0, 4), (1, 4))),
        "down_weight": noise(arg_keys[5], (FF, D), FF ** -0.5, 0.046875, ((0, 4), (1, 4))),
        "proj_input": noise(arg_keys[6], (D, K), D ** -0.5, 0.09375, ((0, 4),)),
        "proj_output": noise(arg_keys[7], (D, K), D ** -0.5, 0.09375, ((0, 4),)),
        "proj_hidden": noise(arg_keys[8], (FF, K), FF ** -0.5, 0.046875, ((0, 4),)),
        "proj_gate": noise(arg_keys[9], (FF, K), FF ** -0.5, 0.046875, ((0, 4),)),
        "proj_up": noise(arg_keys[10], (FF, K), FF ** -0.5, 0.046875, ((0, 4),)),
    }


def outer_sum(selector, left, right):
    weighted = selector[:, :, None] * left[None, :, :]
    return jnp.einsum('eti,tj->eij', weighted, right, precision=lax.Precision.HIGHEST)


def reference(example_blocks, layer_input, out_grad, gate_pre, up_pre, down_weight, proj_input, proj_output, proj_hidden, proj_gate, proj_up):
    shards = EXAMPLES // EX_DEV
    per_shard = SLOTS * BLK
    block_ends = jnp.cumsum(example_blocks.reshape(shards, EX_DEV), axis=1).astype(jnp.int32)
    slot_ids = jnp.arange(SLOTS, dtype=jnp.int32)
    slot_example = jnp.sum((slot_ids[None, :, None] >= block_ends[:, None, :]).astype(jnp.int32), axis=2, dtype=jnp.int32)
    row_example = jnp.repeat(slot_example, BLK, axis=1)
    labels = jnp.arange(EX_DEV, dtype=jnp.int32)

    def one_shard(pair_items):
        shard_index, row_labels = pair_items
        offset = shard_index * per_shard

        def slice_rows(whole):
            return lax.dynamic_slice_in_dim(whole, offset, per_shard, 0)

        inputs = slice_rows(layer_input)
        out_grads = slice_rows(out_grad)
        gate_val = slice_rows(gate_pre).astype(jnp.float32)
        up_val = slice_rows(up_pre).astype(jnp.float32)
        projected_input = jnp.dot(inputs, proj_input, preferred_element_type=jnp.float32).astype(jnp.bfloat16)
        projected_input = lax.optimization_barrier(projected_input).astype(jnp.float32)
        projected_output = jnp.dot(out_grads, proj_output, preferred_element_type=jnp.float32).astype(jnp.bfloat16)
        projected_output = lax.optimization_barrier(projected_output).astype(jnp.float32)
        sigmoid_gate = jax.nn.sigmoid(gate_val)
        hidden = (gate_val * sigmoid_gate * up_val).astype(jnp.bfloat16)
        hidden_grad = jnp.dot(out_grads, down_weight.T, preferred_element_type=jnp.float32)
        gate_grad = (hidden_grad * up_val * sigmoid_gate * (1.0 + gate_val * (1.0 - sigmoid_gate))).astype(jnp.bfloat16)
        up_grad = (hidden_grad * gate_val * sigmoid_gate).astype(jnp.bfloat16)
        hidden_proj = jnp.dot(hidden, proj_hidden, preferred_element_type=jnp.float32)
        gate_proj = jnp.dot(gate_grad, proj_gate, preferred_element_type=jnp.float32)
        up_proj = jnp.dot(up_grad, proj_up, preferred_element_type=jnp.float32)
        selector = (row_labels[None, :] == labels[:, None]).astype(jnp.float32)
        down_part = outer_sum(selector, hidden_proj, projected_output).reshape(EX_DEV, K * K)
        gate_part = outer_sum(selector, projected_input, gate_proj).reshape(EX_DEV, K * K)
        up_part = outer_sum(selector, projected_input, up_proj).reshape(EX_DEV, K * K)
        return jnp.concatenate([down_part, gate_part, up_part], axis=1)

    results = lax.map(one_shard, (jnp.arange(shards, dtype=jnp.int32), row_example))
    return results.reshape(EXAMPLES, 3 * K * K)
```

```python
import jax
import jax.numpy as jnp
from jax import lax
from jax.sharding import PartitionSpec as P

BLK = 24


def example_sums(example_blocks, home_proj, hidden_proj, gate_proj, up_proj):
    rows, rank_dim = hidden_proj.shape
    num_examples = example_blocks.shape[0]
    block_ends = jnp.cumsum(example_blocks) * BLK
    row_ids = jnp.arange(rows, dtype=jnp.int32)
    row_example = jnp.sum(
        (row_ids[:, None] >= block_ends[None, :]).astype(jnp.int32), axis=1, dtype=jnp.int32
    )
    labels = jnp.arange(num_examples, dtype=jnp.int32)
    selector = (row_example[:, None] == labels[None, :]).astype(jnp.float32)
    input_side = home_proj[:, :rank_dim].astype(jnp.float32)
    output_side = home_proj[:, rank_dim:].astype(jnp.float32)

    def spread(left):
        return (selector[:, :, None] * left[:, None, :]).reshape(rows, num_examples * rank_dim)

    def outer(left, right):
        return lax.dot_general(
            left, right, (((0,), (0,)), ((), ())), precision=lax.Precision.HIGHEST
        ).reshape(num_examples, rank_dim, -1)

    down_part = outer(spread(hidden_proj), output_side)
    both = outer(spread(input_side), jnp.concatenate([gate_proj, up_proj], axis=1))
    parts = [down_part, both[:, :, :rank_dim], both[:, :, rank_dim:]]
    summed = jnp.concatenate([p.reshape(num_examples, rank_dim * rank_dim) for p in parts], axis=1)
    return lax.psum_scatter(summed, ("mp", "sub"), scatter_dimension=1, tiled=True)


def home_projections(layer_input, out_grad, proj_input, proj_output):
    home_proj = jnp.concatenate(
        [
            jnp.dot(layer_input, proj_input, preferred_element_type=jnp.float32),
            jnp.dot(out_grad, proj_output, preferred_element_type=jnp.float32),
        ],
        axis=1,
    )
    return lax.psum(home_proj, ("mp", "sub")).astype(jnp.bfloat16)


def body(
    example_blocks,
    layer_input,
    out_grad,
    gate_pre,
    up_pre,
    down_weight,
    proj_input,
    proj_output,
    proj_hidden,
    proj_gate,
    proj_up,
):
    ff_cols = gate_pre.shape[1]
    half = ff_cols // 2
    full_grads = lax.all_gather(out_grad, ("mp", "sub"), axis=1, tiled=True)
    mine = lax.dynamic_slice_in_dim(down_weight, lax.axis_index("groups") * half, half, 0)
    weight_half = lax.all_gather(mine, "dp", axis=1, tiled=True)
    weight = lax.all_gather(weight_half, "groups", axis=0, tiled=True)
    home_proj = home_projections(layer_input, out_grad, proj_input, proj_output)
    hidden_grad = lax.dot_general(
        full_grads, weight, (((1,), (1,)), ((), ())), preferred_element_type=jnp.float32
    )
    gate_val = gate_pre.astype(jnp.float32)
    up_val = up_pre.astype(jnp.float32)
    sigmoid_gate = jax.nn.sigmoid(gate_val)
    hidden = (gate_val * sigmoid_gate * up_val).astype(jnp.bfloat16)
    gate_grad = (
        hidden_grad * up_val * sigmoid_gate * (1.0 + gate_val * (1.0 - sigmoid_gate))
    ).astype(jnp.bfloat16)
    up_grad = (hidden_grad * gate_val * sigmoid_gate).astype(jnp.bfloat16)
    hidden_proj = jnp.dot(hidden, proj_hidden, preferred_element_type=jnp.float32)
    gate_proj = jnp.dot(gate_grad, proj_gate, preferred_element_type=jnp.float32)
    up_proj = jnp.dot(up_grad, proj_up, preferred_element_type=jnp.float32)
    return example_sums(example_blocks, home_proj, hidden_proj, gate_proj, up_proj)


def solution(mesh):
    rows = P(("groups", "dp"), ("mp", "sub"))
    proj = P(("mp", "sub"), None)
    placed = (P(("groups", "dp")),) + (rows,) * 4 + (P(("mp", "sub"), "dp"),) + (proj,) * 5
    return jax.shard_map(
        body, mesh=mesh, in_specs=placed, out_specs=rows, check_vma=False
    )
```

```python
import functools

import jax
import jax.numpy as jnp
from jax import lax
from jax.experimental import pallas as pl
from jax.experimental.pallas import tpu as pltpu
from jax.sharding import PartitionSpec as P

BLK = 24
CHUNK = 256
MESH = pl.DeviceIdType.MESH


def gather_kernel(
    shards,
    feature_shards,
    cores,
    chunks,
    grads_ref,
    gate_ref,
    up_ref,
    weight_ref,
    proj_hidden_ref,
    proj_gate_ref,
    proj_up_ref,
    hidden_out,
    gate_out,
    up_out,
    weights,
    grads,
    grad_send,
    grad_recv,
    local_sem,
    send_right,
    send_left,
    recv_sem,
    group_send,
    group_recv,
):
    group = lax.axis_index("groups")
    here = lax.axis_index("dp")
    feature = lax.axis_index("mp") * cores + lax.axis_index("sub")
    half = chunks * CHUNK
    has_left = here > 0
    has_right = here < shards - 1

    def rows_of(group_at, chunk):
        return pl.ds(pl.multiple_of(group_at * half + chunk * CHUNK, CHUNK), CHUNK)

    def grad_copy(to, origin):
        return pltpu.make_async_remote_copy(
            src_ref=grads_ref,
            dst_ref=grads.at[origin],
            send_sem=grad_send.at[to],
            recv_sem=grad_recv.at[origin],
            device_id={"mp": to // cores, "sub": to % cores},
            device_id_type=MESH,
        )

    def line_copy(source_ref, origin, chunk, to, sems):
        return pltpu.make_async_remote_copy(
            src_ref=source_ref,
            dst_ref=weights.at[origin, rows_of(group, chunk)],
            send_sem=sems.at[origin, chunk],
            recv_sem=recv_sem.at[origin, chunk],
            device_id={"dp": to},
            device_id_type=MESH,
        )

    def group_copy(group_at, origin, chunk):
        block = weights.at[origin, rows_of(group_at, chunk)]
        return pltpu.make_async_remote_copy(
            src_ref=block,
            dst_ref=block,
            send_sem=group_send.at[origin, chunk],
            recv_sem=group_recv.at[origin, chunk],
            device_id={"groups": 1 - group},
            device_id_type=MESH,
        )

    def held(origin, chunk):
        return weights.at[origin, rows_of(group, chunk)]

    barrier = pltpu.get_barrier_semaphore()
    pl.semaphore_signal(barrier, inc=1, device_id={"groups": 1 - group}, device_id_type=MESH)
    for step in range(1, feature_shards):
        to = lax.rem(feature + step, feature_shards)
        pl.semaphore_signal(
            barrier, inc=1, device_id={"mp": to // cores, "sub": to % cores}, device_id_type=MESH
        )

    @pl.when(has_left)
    def _():
        pl.semaphore_signal(barrier, inc=1, device_id={"dp": here - 1}, device_id_type=MESH)

    @pl.when(has_right)
    def _():
        pl.semaphore_signal(barrier, inc=1, device_id={"dp": here + 1}, device_id_type=MESH)

    at_an_end = jnp.logical_or(here == 0, here == shards - 1)

    @pl.when(at_an_end)
    def _():
        pl.semaphore_wait(barrier, feature_shards + 1)

    @pl.when(jnp.logical_not(at_an_end))
    def _():
        pl.semaphore_wait(barrier, feature_shards + 2)

    def send_own(chunk):
        own = weight_ref.at[rows_of(group, chunk)]

        @pl.when(has_right)
        def _():
            line_copy(own, here, chunk, here + 1, send_right).start()

        @pl.when(has_left)
        def _():
            line_copy(own, here, chunk, here - 1, send_left).start()

    send_own(0)
    for step in range(1, feature_shards):
        grad_copy(lax.rem(feature + step, feature_shards), feature).start()
    local_grads = pltpu.make_async_copy(grads_ref, grads.at[feature], local_sem.at[0])
    local_grads.start()
    local_weight = pltpu.make_async_copy(weight_ref, weights.at[here], local_sem.at[1])
    local_weight.start()
    hidden_out[...] = jnp.zeros_like(hidden_out)
    gate_out[...] = jnp.zeros_like(gate_out)
    up_out[...] = jnp.zeros_like(up_out)
    local_grads.wait()
    local_weight.wait()

    def pass_on(origin, chunk, more, to, sems):
        line_copy(held(origin, chunk), origin, chunk, to, sems).wait_recv()

        @pl.when(more)
        def _():
            line_copy(held(origin, chunk), origin, chunk, to, sems).start()

        group_copy(group, origin, chunk).start()

    def work(group_at, chunk):
        span = rows_of(group_at, chunk)
        hidden_grad = jnp.zeros((grads_ref.shape[0], CHUNK), jnp.float32)
        for origin in range(shards):
            hidden_grad += lax.dot_general(
                grads[origin],
                weights[origin, span, :],
                (((1,), (1,)), ((), ())),
                preferred_element_type=jnp.float32,
            )
        gate_val = gate_ref[:, span].astype(jnp.float32)
        up_val = up_ref[:, span].astype(jnp.float32)
        sigmoid_gate = jax.nn.sigmoid(gate_val)
        silu_gate = gate_val * sigmoid_gate
        hidden = (silu_gate * up_val).astype(jnp.bfloat16)
        gate_grad = (
            hidden_grad * up_val * sigmoid_gate * (1.0 + gate_val * (1.0 - sigmoid_gate))
        ).astype(jnp.bfloat16)
        up_grad = (hidden_grad * silu_gate).astype(jnp.bfloat16)
        hidden_out[...] += jnp.dot(
            hidden, proj_hidden_ref[span, :], preferred_element_type=jnp.float32
        )
        gate_out[...] += jnp.dot(
            gate_grad, proj_gate_ref[span, :], preferred_element_type=jnp.float32
        )
        up_out[...] += jnp.dot(up_grad, proj_up_ref[span, :], preferred_element_type=jnp.float32)

    def tick(at, carry):
        @pl.when(at + 1 < chunks)
        def _():
            send_own(at + 1)

        for step in range(1, shards):
            chunk = at - step
            inside = jnp.logical_and(chunk >= 0, chunk < chunks)

            @pl.when(jnp.logical_and(inside, here >= step))
            def _():
                pass_on(here - step, chunk, has_right, here + 1, send_right)

            @pl.when(jnp.logical_and(inside, here + step < shards))
            def _():
                pass_on(here + step, chunk, has_left, here - 1, send_left)

        @pl.when(at == shards - 1)
        def _():
            for step in range(1, feature_shards):
                origin = lax.rem(feature + step, feature_shards)
                grad_copy(origin, origin).wait_recv()

        @pl.when(at >= shards)
        def _():
            for step in range(1, shards):
                group_copy(1 - group, lax.rem(here + step, shards), at - shards).wait_recv()
            work(1 - group, at - shards)

        @pl.when(jnp.logical_and(at >= shards - 1, at < chunks + shards - 1))
        def _():
            work(group, at - shards + 1)

        return carry

    lax.fori_loop(0, chunks + shards, tick, 0)

    for step in range(1, feature_shards):
        grad_copy(lax.rem(feature + step, feature_shards), feature).wait_send()

    def drain(chunk, carry):
        for origin in range(shards):
            @pl.when(jnp.logical_and(has_right, here >= origin))
            def _():
                line_copy(held(origin, chunk), origin, chunk, here + 1, send_right).wait_send()

            @pl.when(jnp.logical_and(has_left, here <= origin))
            def _():
                line_copy(held(origin, chunk), origin, chunk, here - 1, send_left).wait_send()

            @pl.when(here != origin)
            def _():
                group_copy(group, origin, chunk).wait_send()

        return carry

    lax.fori_loop(0, chunks, drain, 0)


def gathered_projections(
    shards, feature_shards, cores, out_grad, gate_pre, up_pre, down_weight, proj_hidden, proj_gate, proj_up
):
    rows, columns = out_grad.shape
    ff_cols = gate_pre.shape[1]
    rank_dim = proj_hidden.shape[1]
    chunks = ff_cols // (2 * CHUNK)
    in_vmem = pl.BlockSpec(memory_space=pltpu.VMEM)
    full = columns * feature_shards
    return pl.pallas_call(
        functools.partial(gather_kernel, shards, feature_shards, cores, chunks),
        out_shape=[jax.ShapeDtypeStruct((rows, rank_dim), jnp.float32)] * 3,
        in_specs=[in_vmem] * 3 + [pl.BlockSpec(memory_space=pl.ANY)] + [in_vmem] * 3,
        out_specs=[in_vmem] * 3,
        scratch_shapes=[
            pltpu.VMEM((shards, ff_cols, columns), jnp.bfloat16),
            pltpu.VMEM((feature_shards, rows, columns), jnp.bfloat16),
            pltpu.SemaphoreType.DMA((feature_shards,)),
            pltpu.SemaphoreType.DMA((feature_shards,)),
            pltpu.SemaphoreType.DMA((2,)),
        ]
        + [pltpu.SemaphoreType.DMA((shards, chunks))] * 5,
        compiler_params=pltpu.CompilerParams(
            collective_id=0, has_side_effects=True, vmem_limit_bytes=60 * 2**20
        ),
        cost_estimate=pl.CostEstimate(
            flops=2 * rows * ff_cols * (full + 3 * rank_dim),
            bytes_accessed=2 * ff_cols * (2 * rows + full),
            transcendentals=rows * ff_cols,
        ),
    )(out_grad, gate_pre, up_pre, down_weight, proj_hidden, proj_gate, proj_up)


def example_sums(example_blocks, home_proj, hidden_proj, gate_proj, up_proj):
    rows, rank_dim = hidden_proj.shape
    num_examples = example_blocks.shape[0]
    block_ends = jnp.cumsum(example_blocks) * BLK
    row_ids = jnp.arange(rows, dtype=jnp.int32)
    row_example = jnp.sum(
        (row_ids[:, None] >= block_ends[None, :]).astype(jnp.int32), axis=1, dtype=jnp.int32
    )
    labels = jnp.arange(num_examples, dtype=jnp.int32)
    selector = (row_example[:, None] == labels[None, :]).astype(jnp.float32)
    input_side = home_proj[:, :rank_dim].astype(jnp.float32)
    output_side = home_proj[:, rank_dim:].astype(jnp.float32)

    def spread(left):
        return (selector[:, :, None] * left[:, None, :]).reshape(rows, num_examples * rank_dim)

    def outer(left, right):
        return lax.dot_general(
            left, right, (((0,), (0,)), ((), ())), precision=lax.Precision.HIGHEST
        ).reshape(num_examples, rank_dim, -1)

    down_part = outer(spread(hidden_proj), output_side)
    both = outer(spread(input_side), jnp.concatenate([gate_proj, up_proj], axis=1))
    parts = [down_part, both[:, :, :rank_dim], both[:, :, rank_dim:]]
    summed = jnp.concatenate([p.reshape(num_examples, rank_dim * rank_dim) for p in parts], axis=1)
    return lax.psum_scatter(summed, ("mp", "sub"), scatter_dimension=1, tiled=True)


def home_projections(layer_input, out_grad, proj_input, proj_output):
    home_proj = jnp.concatenate(
        [
            jnp.dot(layer_input, proj_input, preferred_element_type=jnp.float32),
            jnp.dot(out_grad, proj_output, preferred_element_type=jnp.float32),
        ],
        axis=1,
    )
    return lax.psum(home_proj, ("mp", "sub")).astype(jnp.bfloat16)


def plain_projections(out_grad, gate_pre, up_pre, down_weight, proj_hidden, proj_gate, proj_up):
    pieces = gate_pre.shape[1] // lax.axis_size("groups")
    full_grads = lax.all_gather(out_grad, ("mp", "sub"), axis=1, tiled=True)
    mine = lax.dynamic_slice_in_dim(down_weight, lax.axis_index("groups") * pieces, pieces, 0)
    weight_part = lax.all_gather(mine, "dp", axis=1, tiled=True)
    weight = lax.all_gather(weight_part, "groups", axis=0, tiled=True)
    hidden_grad = lax.dot_general(
        full_grads, weight, (((1,), (1,)), ((), ())), preferred_element_type=jnp.float32
    )
    gate_val = gate_pre.astype(jnp.float32)
    up_val = up_pre.astype(jnp.float32)
    sigmoid_gate = jax.nn.sigmoid(gate_val)
    hidden = (gate_val * sigmoid_gate * up_val).astype(jnp.bfloat16)
    gate_grad = (
        hidden_grad * up_val * sigmoid_gate * (1.0 + gate_val * (1.0 - sigmoid_gate))
    ).astype(jnp.bfloat16)
    up_grad = (hidden_grad * gate_val * sigmoid_gate).astype(jnp.bfloat16)
    return (
        jnp.dot(hidden, proj_hidden, preferred_element_type=jnp.float32),
        jnp.dot(gate_grad, proj_gate, preferred_element_type=jnp.float32),
        jnp.dot(up_grad, proj_up, preferred_element_type=jnp.float32),
    )


def body(
    example_blocks,
    layer_input,
    out_grad,
    gate_pre,
    up_pre,
    down_weight,
    proj_input,
    proj_output,
    proj_hidden,
    proj_gate,
    proj_up,
):
    home_proj = home_projections(layer_input, out_grad, proj_input, proj_output)
    shards = lax.axis_size("dp")
    feature_shards = lax.axis_size("mp") * lax.axis_size("sub")
    even = gate_pre.shape[1] % (2 * CHUNK) == 0 and lax.axis_size("groups") == 2
    if even and shards == feature_shards:
        hidden_proj, gate_proj, up_proj = gathered_projections(
            shards,
            feature_shards,
            lax.axis_size("sub"),
            out_grad,
            gate_pre,
            up_pre,
            down_weight,
            proj_hidden,
            proj_gate,
            proj_up,
        )
    else:
        hidden_proj, gate_proj, up_proj = plain_projections(
            out_grad, gate_pre, up_pre, down_weight, proj_hidden, proj_gate, proj_up
        )
    return example_sums(example_blocks, home_proj, hidden_proj, gate_proj, up_proj)


def solution(mesh):
    rows = P(("groups", "dp"), ("mp", "sub"))
    proj = P(("mp", "sub"), None)
    placed = (P(("groups", "dp")),) + (rows,) * 4 + (P(("mp", "sub"), "dp"),) + (proj,) * 5
    return jax.shard_map(
        body, mesh=mesh, in_specs=placed, out_specs=rows, check_vma=False
    )
```

```python
import functools

import jax
import jax.numpy as jnp
from jax import lax
from jax.experimental import pallas as pl
from jax.experimental.pallas import tpu as pltpu
from jax.sharding import PartitionSpec as P

BLK = 24
CHUNK = 256
MESH = pl.DeviceIdType.MESH


def gather_kernel(
    shards,
    feature_shards,
    cores,
    chunks,
    grads_ref,
    gate_ref,
    up_ref,
    weight_ref,
    proj_hidden_ref,
    proj_gate_ref,
    proj_up_ref,
    inputs_ref,
    proj_input_ref,
    proj_output_ref,
    selector_ref,
    out_ref,
    hidden_out,
    gate_out,
    up_out,
    home_parts,
    sums,
    arrived,
    weights,
    grads,
    grad_send,
    grad_recv,
    local_sem,
    send_right,
    send_left,
    recv_sem,
    group_send,
    group_recv,
    home_send,
    home_recv,
    sums_send,
    sums_recv,
):
    group = lax.axis_index("groups")
    here = lax.axis_index("dp")
    feature = lax.axis_index("mp") * cores + lax.axis_index("sub")
    half = chunks * CHUNK
    has_left = here > 0
    has_right = here < shards - 1

    def rows_of(group_at, chunk):
        return pl.ds(pl.multiple_of(group_at * half + chunk * CHUNK, CHUNK), CHUNK)

    def grad_copy(to, origin):
        return pltpu.make_async_remote_copy(
            src_ref=grads_ref,
            dst_ref=grads.at[origin],
            send_sem=grad_send.at[to],
            recv_sem=grad_recv.at[origin],
            device_id={"mp": to // cores, "sub": to % cores},
            device_id_type=MESH,
        )

    def home_copy(to, origin):
        return pltpu.make_async_remote_copy(
            src_ref=home_parts.at[feature],
            dst_ref=home_parts.at[origin],
            send_sem=home_send.at[to],
            recv_sem=home_recv.at[origin],
            device_id={"mp": to // cores, "sub": to % cores},
            device_id_type=MESH,
        )

    share = arrived.shape[2]

    def share_of(at):
        return pl.ds(pl.multiple_of(at * share, 8), share)

    def sums_copy(to, origin):
        return pltpu.make_async_remote_copy(
            src_ref=sums.at[:, share_of(to), :],
            dst_ref=arrived.at[origin],
            send_sem=sums_send.at[to],
            recv_sem=sums_recv.at[origin],
            device_id={"mp": to // cores, "sub": to % cores},
            device_id_type=MESH,
        )

    def line_copy(source_ref, origin, chunk, to, sems):
        return pltpu.make_async_remote_copy(
            src_ref=source_ref,
            dst_ref=weights.at[origin, rows_of(group, chunk)],
            send_sem=sems.at[origin, chunk],
            recv_sem=recv_sem.at[origin, chunk],
            device_id={"dp": to},
            device_id_type=MESH,
        )

    def group_copy(group_at, origin, chunk):
        block = weights.at[origin, rows_of(group_at, chunk)]
        return pltpu.make_async_remote_copy(
            src_ref=block,
            dst_ref=block,
            send_sem=group_send.at[origin, chunk],
            recv_sem=group_recv.at[origin, chunk],
            device_id={"groups": 1 - group},
            device_id_type=MESH,
        )

    def held(origin, chunk):
        return weights.at[origin, rows_of(group, chunk)]

    barrier = pltpu.get_barrier_semaphore()
    pl.semaphore_signal(barrier, inc=1, device_id={"groups": 1 - group}, device_id_type=MESH)
    for step in range(1, feature_shards):
        to = lax.rem(feature + step, feature_shards)
        pl.semaphore_signal(
            barrier, inc=1, device_id={"mp": to // cores, "sub": to % cores}, device_id_type=MESH
        )

    @pl.when(has_left)
    def _():
        pl.semaphore_signal(barrier, inc=1, device_id={"dp": here - 1}, device_id_type=MESH)

    @pl.when(has_right)
    def _():
        pl.semaphore_signal(barrier, inc=1, device_id={"dp": here + 1}, device_id_type=MESH)

    at_an_end = jnp.logical_or(here == 0, here == shards - 1)

    @pl.when(at_an_end)
    def _():
        pl.semaphore_wait(barrier, feature_shards + 1)

    @pl.when(jnp.logical_not(at_an_end))
    def _():
        pl.semaphore_wait(barrier, feature_shards + 2)

    def send_own(chunk):
        own = weight_ref.at[rows_of(group, chunk)]

        @pl.when(has_right)
        def _():
            line_copy(own, here, chunk, here + 1, send_right).start()

        @pl.when(has_left)
        def _():
            line_copy(own, here, chunk, here - 1, send_left).start()

    send_own(0)
    for step in range(1, feature_shards):
        grad_copy(lax.rem(feature + step, feature_shards), feature).start()
    local_grads = pltpu.make_async_copy(grads_ref, grads.at[feature], local_sem.at[0])
    local_grads.start()
    local_weight = pltpu.make_async_copy(weight_ref, weights.at[here], local_sem.at[1])
    local_weight.start()
    rank_dim = proj_input_ref.shape[0]

    def turned_dot(left, right):
        return lax.dot_general(
            left, right, (((1,), (1,)), ((), ())), preferred_element_type=jnp.float32
        )

    home_parts[feature] = jnp.concatenate(
        [
            turned_dot(inputs_ref[...], proj_input_ref[...]),
            turned_dot(grads_ref[...], proj_output_ref[...]),
        ],
        axis=1,
    )
    for step in range(1, feature_shards):
        home_copy(lax.rem(feature + step, feature_shards), feature).start()
    hidden_out[...] = jnp.zeros_like(hidden_out)
    gate_out[...] = jnp.zeros_like(gate_out)
    up_out[...] = jnp.zeros_like(up_out)
    local_grads.wait()
    local_weight.wait()

    def pass_on(origin, chunk, more, to, sems):
        line_copy(held(origin, chunk), origin, chunk, to, sems).wait_recv()

        @pl.when(more)
        def _():
            line_copy(held(origin, chunk), origin, chunk, to, sems).start()

        group_copy(group, origin, chunk).start()

    def work(group_at, chunk):
        span = rows_of(group_at, chunk)
        hidden_grad = jnp.zeros((grads_ref.shape[0], CHUNK), jnp.float32)
        for origin in range(shards):
            hidden_grad += lax.dot_general(
                grads[origin],
                weights[origin, span, :],
                (((1,), (1,)), ((), ())),
                preferred_element_type=jnp.float32,
            )
        gate_val = gate_ref[:, span].astype(jnp.float32)
        up_val = up_ref[:, span].astype(jnp.float32)
        sigmoid_gate = jax.nn.sigmoid(gate_val)
        silu_gate = gate_val * sigmoid_gate
        hidden = (silu_gate * up_val).astype(jnp.bfloat16)
        gate_grad = (
            hidden_grad * up_val * sigmoid_gate * (1.0 + gate_val * (1.0 - sigmoid_gate))
        ).astype(jnp.bfloat16)
        up_grad = (hidden_grad * silu_gate).astype(jnp.bfloat16)
        hidden_out[...] += turned_dot(hidden, proj_hidden_ref[:, span])
        gate_out[...] += turned_dot(gate_grad, proj_gate_ref[:, span])
        up_out[...] += turned_dot(up_grad, proj_up_ref[:, span])

    def tick(at, carry):
        @pl.when(at + 1 < chunks)
        def _():
            send_own(at + 1)

        for step in range(1, shards):
            chunk = at - step
            inside = jnp.logical_and(chunk >= 0, chunk < chunks)

            @pl.when(jnp.logical_and(inside, here >= step))
            def _():
                pass_on(here - step, chunk, has_right, here + 1, send_right)

            @pl.when(jnp.logical_and(inside, here + step < shards))
            def _():
                pass_on(here + step, chunk, has_left, here - 1, send_left)

        @pl.when(at == shards - 1)
        def _():
            for step in range(1, feature_shards):
                origin = lax.rem(feature + step, feature_shards)
                grad_copy(origin, origin).wait_recv()

        @pl.when(at >= shards)
        def _():
            for step in range(1, shards):
                group_copy(1 - group, lax.rem(here + step, shards), at - shards).wait_recv()
            work(1 - group, at - shards)

        @pl.when(jnp.logical_and(at >= shards - 1, at < chunks + shards - 1))
        def _():
            work(group, at - shards + 1)

        return carry

    lax.fori_loop(0, chunks + shards, tick, 0)

    for step in range(1, feature_shards):
        origin = lax.rem(feature + step, feature_shards)
        home_copy(origin, origin).wait_recv()
        home_copy(origin, feature).wait_send()
    home = home_parts[0]
    for origin in range(1, feature_shards):
        home += home_parts[origin]
    home = home.astype(jnp.bfloat16).astype(jnp.float32)
    input_side, output_side = home[:, :rank_dim], home[:, rank_dim:]
    num_examples = sums.shape[0]

    def outer(left, right):
        return lax.dot_general(
            left,
            right,
            (((0,), (0,)), ((), ())),
            precision=lax.Precision.HIGHEST,
            preferred_element_type=jnp.float32,
        )

    for example in range(num_examples):
        chosen = selector_ref[:, example : example + 1]
        sums[example, :rank_dim, :] = outer(hidden_out[...] * chosen, output_side)
        left = input_side * chosen
        sums[example, rank_dim : 2 * rank_dim, :] = outer(left, gate_out[...])
        sums[example, 2 * rank_dim :, :] = outer(left, up_out[...])
    for step in range(1, feature_shards):
        sums_copy(lax.rem(feature + step, feature_shards), feature).start()
    out_ref[...] = sums[:, share_of(feature), :]
    for step in range(1, feature_shards):
        origin = lax.rem(feature + step, feature_shards)
        sums_copy(origin, origin).wait_recv()
        out_ref[...] += arrived[origin]
    for step in range(1, feature_shards):
        sums_copy(lax.rem(feature + step, feature_shards), feature).wait_send()

    for step in range(1, feature_shards):
        grad_copy(lax.rem(feature + step, feature_shards), feature).wait_send()

    def drain(chunk, carry):
        for origin in range(shards):
            @pl.when(jnp.logical_and(has_right, here >= origin))
            def _():
                line_copy(held(origin, chunk), origin, chunk, here + 1, send_right).wait_send()

            @pl.when(jnp.logical_and(has_left, here <= origin))
            def _():
                line_copy(held(origin, chunk), origin, chunk, here - 1, send_left).wait_send()

            @pl.when(here != origin)
            def _():
                group_copy(group, origin, chunk).wait_send()

        return carry

    lax.fori_loop(0, chunks, drain, 0)


def gathered_sums(
    shards, feature_shards, cores, example_blocks, layer_input, out_grad, gate_pre, up_pre, down_weight, projections
):
    rows, columns = out_grad.shape
    ff_cols = gate_pre.shape[1]
    rank_dim = projections[0].shape[1]
    num_examples = example_blocks.shape[0]
    chunks = ff_cols // (2 * CHUNK)
    share = 3 * rank_dim // feature_shards
    in_vmem = pl.BlockSpec(memory_space=pltpu.VMEM)
    full = columns * feature_shards
    turned = [projection.T for projection in projections]
    summed = pl.pallas_call(
        functools.partial(gather_kernel, shards, feature_shards, cores, chunks),
        out_shape=jax.ShapeDtypeStruct((num_examples, share, rank_dim), jnp.float32),
        in_specs=[in_vmem] * 3 + [pl.BlockSpec(memory_space=pl.ANY)] + [in_vmem] * 7,
        out_specs=in_vmem,
        scratch_shapes=[pltpu.VMEM((rows, rank_dim), jnp.float32)] * 3
        + [
            pltpu.VMEM((feature_shards, rows, 2 * rank_dim), jnp.float32),
            pltpu.VMEM((num_examples, 3 * rank_dim, rank_dim), jnp.float32),
            pltpu.VMEM((feature_shards, num_examples, share, rank_dim), jnp.float32),
            pltpu.VMEM((shards, ff_cols, columns), jnp.bfloat16),
            pltpu.VMEM((feature_shards, rows, columns), jnp.bfloat16),
            pltpu.SemaphoreType.DMA((feature_shards,)),
            pltpu.SemaphoreType.DMA((feature_shards,)),
            pltpu.SemaphoreType.DMA((2,)),
        ]
        + [pltpu.SemaphoreType.DMA((shards, chunks))] * 5
        + [pltpu.SemaphoreType.DMA((feature_shards,))] * 4,
        compiler_params=pltpu.CompilerParams(
            collective_id=0, has_side_effects=True, vmem_limit_bytes=62 * 2**20
        ),
        cost_estimate=pl.CostEstimate(
            flops=2 * rows * ff_cols * (full + 3 * rank_dim),
            bytes_accessed=2 * ff_cols * (2 * rows + full),
            transcendentals=rows * ff_cols,
        ),
    )(
        out_grad,
        gate_pre,
        up_pre,
        down_weight,
        *turned[2:],
        layer_input,
        *turned[:2],
        row_selector(example_blocks, rows),
    )
    return summed.reshape(num_examples, share * rank_dim)


def row_selector(example_blocks, rows):
    num_examples = example_blocks.shape[0]
    labels = jnp.arange(num_examples, dtype=jnp.int32)
    earlier = (labels[:, None] <= labels[None, :]).astype(jnp.int32)
    block_ends = jnp.sum(example_blocks[:, None] * earlier, axis=0) * BLK
    row_ids = jnp.arange(rows, dtype=jnp.int32)[:, None]
    inside = (row_ids < block_ends[None, :]) & (row_ids >= (block_ends - example_blocks * BLK)[None, :])
    return inside.astype(jnp.float32)


def example_sums(example_blocks, home_proj, hidden_proj, gate_proj, up_proj):
    rows, rank_dim = hidden_proj.shape
    num_examples = example_blocks.shape[0]
    selector = row_selector(example_blocks, rows)
    input_side = home_proj[:, :rank_dim].astype(jnp.float32)
    output_side = home_proj[:, rank_dim:].astype(jnp.float32)

    def spread(left):
        return (selector[:, :, None] * left[:, None, :]).reshape(rows, num_examples * rank_dim)

    def outer(left, right):
        return lax.dot_general(
            left, right, (((0,), (0,)), ((), ())), precision=lax.Precision.HIGHEST
        ).reshape(num_examples, rank_dim, -1)

    down_part = outer(spread(hidden_proj), output_side)
    both = outer(spread(input_side), jnp.concatenate([gate_proj, up_proj], axis=1))
    parts = [down_part, both[:, :, :rank_dim], both[:, :, rank_dim:]]
    summed = jnp.concatenate([p.reshape(num_examples, rank_dim * rank_dim) for p in parts], axis=1)
    return lax.psum_scatter(summed, ("mp", "sub"), scatter_dimension=1, tiled=True)


def home_projections(layer_input, out_grad, proj_input, proj_output):
    home_proj = jnp.concatenate(
        [
            jnp.dot(layer_input, proj_input, preferred_element_type=jnp.float32),
            jnp.dot(out_grad, proj_output, preferred_element_type=jnp.float32),
        ],
        axis=1,
    )
    return lax.psum(home_proj, ("mp", "sub")).astype(jnp.bfloat16)


def plain_projections(out_grad, gate_pre, up_pre, down_weight, proj_hidden, proj_gate, proj_up):
    pieces = gate_pre.shape[1] // lax.axis_size("groups")
    full_grads = lax.all_gather(out_grad, ("mp", "sub"), axis=1, tiled=True)
    mine = lax.dynamic_slice_in_dim(down_weight, lax.axis_index("groups") * pieces, pieces, 0)
    weight_part = lax.all_gather(mine, "dp", axis=1, tiled=True)
    weight = lax.all_gather(weight_part, "groups", axis=0, tiled=True)
    hidden_grad = lax.dot_general(
        full_grads, weight, (((1,), (1,)), ((), ())), preferred_element_type=jnp.float32
    )
    gate_val = gate_pre.astype(jnp.float32)
    up_val = up_pre.astype(jnp.float32)
    sigmoid_gate = jax.nn.sigmoid(gate_val)
    hidden = (gate_val * sigmoid_gate * up_val).astype(jnp.bfloat16)
    gate_grad = (
        hidden_grad * up_val * sigmoid_gate * (1.0 + gate_val * (1.0 - sigmoid_gate))
    ).astype(jnp.bfloat16)
    up_grad = (hidden_grad * gate_val * sigmoid_gate).astype(jnp.bfloat16)
    return (
        jnp.dot(hidden, proj_hidden, preferred_element_type=jnp.float32),
        jnp.dot(gate_grad, proj_gate, preferred_element_type=jnp.float32),
        jnp.dot(up_grad, proj_up, preferred_element_type=jnp.float32),
    )


def body(
    example_blocks,
    layer_input,
    out_grad,
    gate_pre,
    up_pre,
    down_weight,
    proj_input,
    proj_output,
    proj_hidden,
    proj_gate,
    proj_up,
):
    shards = lax.axis_size("dp")
    feature_shards = lax.axis_size("mp") * lax.axis_size("sub")
    even = gate_pre.shape[1] % (2 * CHUNK) == 0 and lax.axis_size("groups") == 2
    even = even and (3 * proj_up.shape[1]) % (8 * feature_shards) == 0
    if even and shards == feature_shards:
        return gathered_sums(
            shards,
            feature_shards,
            lax.axis_size("sub"),
            example_blocks,
            layer_input,
            out_grad,
            gate_pre,
            up_pre,
            down_weight,
            (proj_input, proj_output, proj_hidden, proj_gate, proj_up),
        )
    home_proj = home_projections(layer_input, out_grad, proj_input, proj_output)
    hidden_proj, gate_proj, up_proj = plain_projections(
        out_grad, gate_pre, up_pre, down_weight, proj_hidden, proj_gate, proj_up
    )
    return example_sums(example_blocks, home_proj, hidden_proj, gate_proj, up_proj)


def solution(mesh):
    rows = P(("groups", "dp"), ("mp", "sub"))
    proj = P(("mp", "sub"), None)
    placed = (P(("groups", "dp")),) + (rows,) * 4 + (P(("mp", "sub"), "dp"),) + (proj,) * 5
    return jax.shard_map(
        body, mesh=mesh, in_specs=placed, out_specs=rows, check_vma=False
    )
```

```python
import functools

import jax
import jax.numpy as jnp
from jax import lax
from jax.experimental import pallas as pl
from jax.experimental.pallas import tpu as pltpu
from jax.sharding import PartitionSpec as P

BLK = 24
CHUNK = 256
MESH = pl.DeviceIdType.MESH


def gather_kernel(
    shards,
    feature_shards,
    cores,
    chunks,
    grads_ref,
    gate_ref,
    up_ref,
    weight_ref,
    proj_hidden_ref,
    proj_gate_ref,
    proj_up_ref,
    inputs_ref,
    proj_input_ref,
    proj_output_ref,
    selector_ref,
    out_ref,
    hidden_out,
    gate_out,
    up_out,
    home_parts,
    sums,
    arrived,
    weights,
    grads,
    grad_send,
    grad_recv,
    local_sem,
    send_right,
    send_left,
    recv_sem,
    group_send,
    group_recv,
    home_send,
    home_recv,
    sums_send,
    sums_recv,
):
    group = lax.axis_index("groups")
    here = lax.axis_index("dp")
    feature = lax.axis_index("mp") * cores + lax.axis_index("sub")
    half = chunks * CHUNK
    has_left = here > 0
    has_right = here < shards - 1

    def rows_of(group_at, chunk):
        return pl.ds(pl.multiple_of(group_at * half + chunk * CHUNK, CHUNK), CHUNK)

    def grad_copy(to, origin):
        return pltpu.make_async_remote_copy(
            src_ref=grads_ref,
            dst_ref=grads.at[origin],
            send_sem=grad_send.at[to],
            recv_sem=grad_recv.at[origin],
            device_id={"mp": to // cores, "sub": to % cores},
            device_id_type=MESH,
        )

    def home_copy(to, origin):
        return pltpu.make_async_remote_copy(
            src_ref=home_parts.at[feature],
            dst_ref=home_parts.at[origin],
            send_sem=home_send.at[to],
            recv_sem=home_recv.at[origin],
            device_id={"mp": to // cores, "sub": to % cores},
            device_id_type=MESH,
        )

    share = arrived.shape[2]

    def share_of(at):
        return pl.ds(pl.multiple_of(at * share, 8), share)

    def sums_copy(to, origin):
        return pltpu.make_async_remote_copy(
            src_ref=sums.at[:, share_of(to), :],
            dst_ref=arrived.at[origin],
            send_sem=sums_send.at[to],
            recv_sem=sums_recv.at[origin],
            device_id={"mp": to // cores, "sub": to % cores},
            device_id_type=MESH,
        )

    def line_copy(source_ref, origin, chunk, to, sems):
        return pltpu.make_async_remote_copy(
            src_ref=source_ref,
            dst_ref=weights.at[origin, rows_of(group, chunk)],
            send_sem=sems.at[origin, chunk],
            recv_sem=recv_sem.at[origin, chunk],
            device_id={"dp": to},
            device_id_type=MESH,
        )

    def group_copy(group_at, origin, chunk):
        block = weights.at[origin, rows_of(group_at, chunk)]
        return pltpu.make_async_remote_copy(
            src_ref=block,
            dst_ref=block,
            send_sem=group_send.at[origin, chunk],
            recv_sem=group_recv.at[origin, chunk],
            device_id={"groups": 1 - group},
            device_id_type=MESH,
        )

    def held(origin, chunk):
        return weights.at[origin, rows_of(group, chunk)]

    barrier = pltpu.get_barrier_semaphore()
    pl.semaphore_signal(barrier, inc=1, device_id={"groups": 1 - group}, device_id_type=MESH)
    for step in range(1, feature_shards):
        to = lax.rem(feature + step, feature_shards)
        pl.semaphore_signal(
            barrier, inc=1, device_id={"mp": to // cores, "sub": to % cores}, device_id_type=MESH
        )

    @pl.when(has_left)
    def _():
        pl.semaphore_signal(barrier, inc=1, device_id={"dp": here - 1}, device_id_type=MESH)

    @pl.when(has_right)
    def _():
        pl.semaphore_signal(barrier, inc=1, device_id={"dp": here + 1}, device_id_type=MESH)

    at_an_end = jnp.logical_or(here == 0, here == shards - 1)

    @pl.when(at_an_end)
    def _():
        pl.semaphore_wait(barrier, feature_shards + 1)

    @pl.when(jnp.logical_not(at_an_end))
    def _():
        pl.semaphore_wait(barrier, feature_shards + 2)

    def send_own(chunk):
        own = weight_ref.at[rows_of(group, chunk)]

        @pl.when(has_right)
        def _():
            line_copy(own, here, chunk, here + 1, send_right).start()

        @pl.when(has_left)
        def _():
            line_copy(own, here, chunk, here - 1, send_left).start()

    send_own(0)
    send_own(1)
    for step in range(1, feature_shards):
        grad_copy(lax.rem(feature + step, feature_shards), feature).start()
    local_grads = pltpu.make_async_copy(grads_ref, grads.at[feature], local_sem.at[0])
    local_grads.start()
    local_weight = pltpu.make_async_copy(weight_ref, weights.at[here], local_sem.at[1])
    local_weight.start()
    rank_dim = proj_input_ref.shape[0]

    def turned_dot(left, right):
        return lax.dot_general(
            left, right, (((1,), (1,)), ((), ())), preferred_element_type=jnp.float32
        )

    home_parts[feature] = jnp.concatenate(
        [
            turned_dot(inputs_ref[...], proj_input_ref[...]),
            turned_dot(grads_ref[...], proj_output_ref[...]),
        ],
        axis=1,
    )
    for step in range(1, feature_shards):
        home_copy(lax.rem(feature + step, feature_shards), feature).start()
    hidden_out[...] = jnp.zeros_like(hidden_out)
    gate_out[...] = jnp.zeros_like(gate_out)
    up_out[...] = jnp.zeros_like(up_out)
    local_grads.wait()
    local_weight.wait()

    def pass_on(origin, chunk, more, to, sems):
        line_copy(held(origin, chunk), origin, chunk, to, sems).wait_recv()

        @pl.when(more)
        def _():
            line_copy(held(origin, chunk), origin, chunk, to, sems).start()

        group_copy(group, origin, chunk).start()

    def work(group_at, chunk):
        span = rows_of(group_at, chunk)
        hidden_grad = jnp.zeros((grads_ref.shape[0], CHUNK), jnp.float32)
        for origin in range(shards):
            hidden_grad += lax.dot_general(
                grads[origin],
                weights[origin, span, :],
                (((1,), (1,)), ((), ())),
                preferred_element_type=jnp.float32,
            )
        gate_val = gate_ref[:, span].astype(jnp.float32)
        up_val = up_ref[:, span].astype(jnp.float32)
        sigmoid_gate = jax.nn.sigmoid(gate_val)
        silu_gate = gate_val * sigmoid_gate
        hidden = (silu_gate * up_val).astype(jnp.bfloat16)
        gate_grad = (
            hidden_grad * up_val * sigmoid_gate * (1.0 + gate_val * (1.0 - sigmoid_gate))
        ).astype(jnp.bfloat16)
        up_grad = (hidden_grad * silu_gate).astype(jnp.bfloat16)
        hidden_out[...] += turned_dot(hidden, proj_hidden_ref[:, span])
        gate_out[...] += turned_dot(gate_grad, proj_gate_ref[:, span])
        up_out[...] += turned_dot(up_grad, proj_up_ref[:, span])

    def tick(at, carry):
        @pl.when(at + 2 < chunks)
        def _():
            send_own(at + 2)

        for step in range(1, shards):
            chunk = at - step
            inside = jnp.logical_and(chunk >= 0, chunk < chunks)

            @pl.when(jnp.logical_and(inside, here >= step))
            def _():
                pass_on(here - step, chunk, has_right, here + 1, send_right)

            @pl.when(jnp.logical_and(inside, here + step < shards))
            def _():
                pass_on(here + step, chunk, has_left, here - 1, send_left)

        @pl.when(at == shards - 1)
        def _():
            for step in range(1, feature_shards):
                origin = lax.rem(feature + step, feature_shards)
                grad_copy(origin, origin).wait_recv()

        @pl.when(at >= shards)
        def _():
            for step in range(1, shards):
                group_copy(1 - group, lax.rem(here + step, shards), at - shards).wait_recv()
            work(1 - group, at - shards)

        @pl.when(jnp.logical_and(at >= shards - 1, at < chunks + shards - 1))
        def _():
            work(group, at - shards + 1)

        return carry

    lax.fori_loop(0, chunks + shards, tick, 0)

    for step in range(1, feature_shards):
        origin = lax.rem(feature + step, feature_shards)
        home_copy(origin, origin).wait_recv()
        home_copy(origin, feature).wait_send()
    home = home_parts[0]
    for origin in range(1, feature_shards):
        home += home_parts[origin]
    home = home.astype(jnp.bfloat16).astype(jnp.float32)
    input_side, output_side = home[:, :rank_dim], home[:, rank_dim:]
    num_examples = sums.shape[0]

    def outer(left, right):
        return lax.dot_general(
            left,
            right,
            (((0,), (0,)), ((), ())),
            precision=lax.Precision.HIGHEST,
            preferred_element_type=jnp.float32,
        )

    for example in range(num_examples):
        chosen = selector_ref[:, example : example + 1]
        sums[example, :rank_dim, :] = outer(hidden_out[...] * chosen, output_side)
        left = input_side * chosen
        sums[example, rank_dim : 2 * rank_dim, :] = outer(left, gate_out[...])
        sums[example, 2 * rank_dim :, :] = outer(left, up_out[...])
    for step in range(1, feature_shards):
        sums_copy(lax.rem(feature + step, feature_shards), feature).start()
    out_ref[...] = sums[:, share_of(feature), :]
    for step in range(1, feature_shards):
        origin = lax.rem(feature + step, feature_shards)
        sums_copy(origin, origin).wait_recv()
        out_ref[...] += arrived[origin]
    for step in range(1, feature_shards):
        sums_copy(lax.rem(feature + step, feature_shards), feature).wait_send()

    for step in range(1, feature_shards):
        grad_copy(lax.rem(feature + step, feature_shards), feature).wait_send()

    def drain(chunk, carry):
        for origin in range(shards):
            @pl.when(jnp.logical_and(has_right, here >= origin))
            def _():
                line_copy(held(origin, chunk), origin, chunk, here + 1, send_right).wait_send()

            @pl.when(jnp.logical_and(has_left, here <= origin))
            def _():
                line_copy(held(origin, chunk), origin, chunk, here - 1, send_left).wait_send()

            @pl.when(here != origin)
            def _():
                group_copy(group, origin, chunk).wait_send()

        return carry

    lax.fori_loop(0, chunks, drain, 0)


def gathered_sums(
    shards, feature_shards, cores, example_blocks, layer_input, out_grad, gate_pre, up_pre, down_weight, projections
):
    rows, columns = out_grad.shape
    ff_cols = gate_pre.shape[1]
    rank_dim = projections[0].shape[1]
    num_examples = example_blocks.shape[0]
    chunks = ff_cols // (2 * CHUNK)
    share = 3 * rank_dim // feature_shards
    in_vmem = pl.BlockSpec(memory_space=pltpu.VMEM)
    full = columns * feature_shards
    turned = [projection.T for projection in projections]
    summed = pl.pallas_call(
        functools.partial(gather_kernel, shards, feature_shards, cores, chunks),
        out_shape=jax.ShapeDtypeStruct((num_examples, share, rank_dim), jnp.float32),
        in_specs=[in_vmem] * 3 + [pl.BlockSpec(memory_space=pl.ANY)] + [in_vmem] * 7,
        out_specs=in_vmem,
        scratch_shapes=[pltpu.VMEM((rows, rank_dim), jnp.float32)] * 3
        + [
            pltpu.VMEM((feature_shards, rows, 2 * rank_dim), jnp.float32),
            pltpu.VMEM((num_examples, 3 * rank_dim, rank_dim), jnp.float32),
            pltpu.VMEM((feature_shards, num_examples, share, rank_dim), jnp.float32),
            pltpu.VMEM((shards, ff_cols, columns), jnp.bfloat16),
            pltpu.VMEM((feature_shards, rows, columns), jnp.bfloat16),
            pltpu.SemaphoreType.DMA((feature_shards,)),
            pltpu.SemaphoreType.DMA((feature_shards,)),
            pltpu.SemaphoreType.DMA((2,)),
        ]
        + [pltpu.SemaphoreType.DMA((shards, chunks))] * 5
        + [pltpu.SemaphoreType.DMA((feature_shards,))] * 4,
        compiler_params=pltpu.CompilerParams(
            collective_id=0, has_side_effects=True, vmem_limit_bytes=62 * 2**20
        ),
        cost_estimate=pl.CostEstimate(
            flops=2 * rows * ff_cols * (full + 3 * rank_dim),
            bytes_accessed=2 * ff_cols * (2 * rows + full),
            transcendentals=rows * ff_cols,
        ),
    )(
        out_grad,
        gate_pre,
        up_pre,
        down_weight,
        *turned[2:],
        layer_input,
        *turned[:2],
        row_selector(example_blocks, rows),
    )
    return summed.reshape(num_examples, share * rank_dim)


def row_selector(example_blocks, rows):
    num_examples = example_blocks.shape[0]
    labels = jnp.arange(num_examples, dtype=jnp.int32)
    earlier = (labels[:, None] <= labels[None, :]).astype(jnp.int32)
    block_ends = jnp.sum(example_blocks[:, None] * earlier, axis=0) * BLK
    row_ids = jnp.arange(rows, dtype=jnp.int32)[:, None]
    inside = (row_ids < block_ends[None, :]) & (row_ids >= (block_ends - example_blocks * BLK)[None, :])
    return inside.astype(jnp.float32)


def example_sums(example_blocks, home_proj, hidden_proj, gate_proj, up_proj):
    rows, rank_dim = hidden_proj.shape
    num_examples = example_blocks.shape[0]
    selector = row_selector(example_blocks, rows)
    input_side = home_proj[:, :rank_dim].astype(jnp.float32)
    output_side = home_proj[:, rank_dim:].astype(jnp.float32)

    def spread(left):
        return (selector[:, :, None] * left[:, None, :]).reshape(rows, num_examples * rank_dim)

    def outer(left, right):
        return lax.dot_general(
            left, right, (((0,), (0,)), ((), ())), precision=lax.Precision.HIGHEST
        ).reshape(num_examples, rank_dim, -1)

    down_part = outer(spread(hidden_proj), output_side)
    both = outer(spread(input_side), jnp.concatenate([gate_proj, up_proj], axis=1))
    parts = [down_part, both[:, :, :rank_dim], both[:, :, rank_dim:]]
    summed = jnp.concatenate([p.reshape(num_examples, rank_dim * rank_dim) for p in parts], axis=1)
    return lax.psum_scatter(summed, ("mp", "sub"), scatter_dimension=1, tiled=True)


def home_projections(layer_input, out_grad, proj_input, proj_output):
    home_proj = jnp.concatenate(
        [
            jnp.dot(layer_input, proj_input, preferred_element_type=jnp.float32),
            jnp.dot(out_grad, proj_output, preferred_element_type=jnp.float32),
        ],
        axis=1,
    )
    return lax.psum(home_proj, ("mp", "sub")).astype(jnp.bfloat16)


def plain_projections(out_grad, gate_pre, up_pre, down_weight, proj_hidden, proj_gate, proj_up):
    pieces = gate_pre.shape[1] // lax.axis_size("groups")
    full_grads = lax.all_gather(out_grad, ("mp", "sub"), axis=1, tiled=True)
    mine = lax.dynamic_slice_in_dim(down_weight, lax.axis_index("groups") * pieces, pieces, 0)
    weight_part = lax.all_gather(mine, "dp", axis=1, tiled=True)
    weight = lax.all_gather(weight_part, "groups", axis=0, tiled=True)
    hidden_grad = lax.dot_general(
        full_grads, weight, (((1,), (1,)), ((), ())), preferred_element_type=jnp.float32
    )
    gate_val = gate_pre.astype(jnp.float32)
    up_val = up_pre.astype(jnp.float32)
    sigmoid_gate = jax.nn.sigmoid(gate_val)
    hidden = (gate_val * sigmoid_gate * up_val).astype(jnp.bfloat16)
    gate_grad = (
        hidden_grad * up_val * sigmoid_gate * (1.0 + gate_val * (1.0 - sigmoid_gate))
    ).astype(jnp.bfloat16)
    up_grad = (hidden_grad * gate_val * sigmoid_gate).astype(jnp.bfloat16)
    return (
        jnp.dot(hidden, proj_hidden, preferred_element_type=jnp.float32),
        jnp.dot(gate_grad, proj_gate, preferred_element_type=jnp.float32),
        jnp.dot(up_grad, proj_up, preferred_element_type=jnp.float32),
    )


def body(
    example_blocks,
    layer_input,
    out_grad,
    gate_pre,
    up_pre,
    down_weight,
    proj_input,
    proj_output,
    proj_hidden,
    proj_gate,
    proj_up,
):
    shards = lax.axis_size("dp")
    feature_shards = lax.axis_size("mp") * lax.axis_size("sub")
    even = gate_pre.shape[1] % (2 * CHUNK) == 0 and lax.axis_size("groups") == 2
    even = even and gate_pre.shape[1] >= 4 * CHUNK and (3 * proj_up.shape[1]) % (8 * feature_shards) == 0
    if even and shards == feature_shards:
        return gathered_sums(
            shards,
            feature_shards,
            lax.axis_size("sub"),
            example_blocks,
            layer_input,
            out_grad,
            gate_pre,
            up_pre,
            down_weight,
            (proj_input, proj_output, proj_hidden, proj_gate, proj_up),
        )
    home_proj = home_projections(layer_input, out_grad, proj_input, proj_output)
    hidden_proj, gate_proj, up_proj = plain_projections(
        out_grad, gate_pre, up_pre, down_weight, proj_hidden, proj_gate, proj_up
    )
    return example_sums(example_blocks, home_proj, hidden_proj, gate_proj, up_proj)


def solution(mesh):
    rows = P(("groups", "dp"), ("mp", "sub"))
    proj = P(("mp", "sub"), None)
    placed = (P(("groups", "dp")),) + (rows,) * 4 + (P(("mp", "sub"), "dp"),) + (proj,) * 5
    return jax.shard_map(
        body, mesh=mesh, in_specs=placed, out_specs=rows, check_vma=False
    )
```
